256 devices in a mesh: section: 4 (over x), ctx: 32 (over z, y), tp: 2 (over core).
Axes of the slice: x: 4, y: 4, z: 8, core: 2. Of those that a mesh axis runs over, the one named last changes fastest.
Arguments:
- queries: bfloat16 [4, 8192, 64, 128], P('section', 'ctx', 'tp'), may hold values from -6 to 6
- key_heads: bfloat16 [4, 8192, 8, 128], P('section', 'ctx', 'tp'), may hold values from -6 to 6
- section_values: bfloat16 [4, 8192, 8, 128], P('section', 'ctx', 'tp'), may hold values from -6 to 6
- block_docs: int32 [64], replicated, may hold values from 0 to 15, never falling along the last dimension, each value on 1 to 15 neighbouring positions
Outputs:
- handed: bfloat16 [4, 8192, 8192], P('section', 'ctx', 'tp')
The draws below stay inside these ranges and needn't reach their ends.
Inputs may be any that keep to these rules, and one draw needn't show every extreme that they name: `block_docs`: numbers never fall along the sequence; every document covers 1 to 15 consecutive blocks and one covers exactly 15.
All inputs are finite; a program needn't handle non-finite values.
Results may differ from the reference program's by a relative error of at most 0.004.
Values may be sent and summed in bfloat16 or wider, within the bound.
A program may use at most 128 MiB of HBM per device.

```python
import math
import jax
import jax.numpy as jnp
import numpy as np
from jax import lax

QUERY_HEADS = 64
KEY_VALUE_HEADS = 8
HEAD_SIZE = 128
TOK_DEV = 256
BLK = 128
SPAN = 8
RELAY_SECTIONS = 4
PACKED_TOKENS = 8192
NBLK = 64
MOST_BLK = 15
DOCS = 16
N_CTX = 32


def draw_queries(key, part):
    key = jax.random.fold_in(key, 11)
    complete_shape = (RELAY_SECTIONS, PACKED_TOKENS, QUERY_HEADS, HEAD_SIZE)
    values_drawn = jax.random.truncated_normal(key, -4.0, 4.0, complete_shape, jnp.float32)
    return values_drawn.astype(jnp.bfloat16)


def draw_key_heads(key, part):
    key = jax.random.fold_in(key, 23)
    complete_shape = (RELAY_SECTIONS, PACKED_TOKENS, KEY_VALUE_HEADS, HEAD_SIZE)
    values_drawn = jax.random.truncated_normal(key, -4.0, 4.0, complete_shape, jnp.float32)
    return values_drawn.astype(jnp.bfloat16)


def block_levels(key, dims, shards, low, top_value):
    def one(dim, parts):
        steps = jax.random.uniform(jax.random.fold_in(jax.random.fold_in(key, 6), dim), (parts,), jnp.float32, low / len(shards), top_value / len(shards))
        return jnp.repeat(jnp.exp(steps), dims[dim] // parts).reshape((-1,) + (1,) * (len(dims) - dim - 1))

    gain = one(*shards[0])
    for cut in shards[1:]:
        gain = gain * one(*cut)
    return gain


def length_profile(number_of, total, reach, lean):
    weights = [(1 << 20) // math.isqrt(grade ** lean) + 1 for grade in range(2, number_of + 1)]
    spare, holding = total - reach - (number_of - 1), [1] * (number_of - 1)
    while spare > 0:
        candidates = [i for i in range(number_of - 1) if holding[i] < reach]
        pool, remaining = sum([weights[i] for i in candidates]), spare
        for i in candidates:
            extra = min(reach - holding[i], max(1, remaining * weights[i] // pool), spare)
            holding[i] = holding[i] + extra
            spare = spare - extra
    return np.array([reach] + holding)


def ragged(rng, number_of, total, limit, skew):
    if number_of == 2:
        one = jax.random.randint(rng, (), max(1, total - limit), min(limit, total - 1) + 1)
        return jnp.stack([one, total - one])
    sizes = jnp.asarray(length_profile(number_of, total, limit, skew), jnp.int32)
    couples = (number_of - 1) // 2
    donor, sink = sizes[1:1 + 2 * couples:2], sizes[2:2 + 2 * couples:2]
    slack = jnp.minimum(donor - 1, limit - sink)
    passed = jax.random.randint(jax.random.fold_in(rng, 1), (couples,), 0, 1 << 20) % (slack + 1)
    sizes = sizes.at[1:1 + 2 * couples:2].set(donor - passed).at[2:2 + 2 * couples:2].set(sink + passed)
    return sizes[jax.random.permutation(jax.random.fold_in(rng, 2), number_of)]


def normal_values(stream_key, dims, width, most, shards=(), held_as=jnp.bfloat16):
    result = jax.random.normal(stream_key, dims, jnp.float32) * width
    if len(shards) > 0:
        result = block_levels(stream_key, dims, shards, -0.22, 0.18) * result
    return jnp.clip(result, min=-most, max=most).astype(held_as)


def setup_inputs(seed: int = 0) -> dict:
    streams_of = jax.random.split(jax.random.key(seed), 5)
    return {
        "queries": draw_queries(jax.random.fold_in(streams_of[4], 71), 0),
        "key_heads": draw_key_heads(jax.random.fold_in(streams_of[4], 71), 0),
        "section_values": normal_values(streams_of[2], (RELAY_SECTIONS, PACKED_TOKENS, KEY_VALUE_HEADS, HEAD_SIZE), 1.0, 6.0, ((0, 4), (1, 32), (2, 2))),
        "block_docs": jnp.searchsorted(jnp.cumsum(ragged(streams_of[3], DOCS, NBLK, MOST_BLK, 2)), jnp.arange(NBLK), side="right").astype(jnp.int32),
    }


LOW_SCORE = -1e+30

def block_attention(query_matrix, key_rows, value_rows, query_docs, key_docs, query_spots, key_spots):
    count_of_rows = query_matrix.shape[0]
    group_width = QUERY_HEADS // KEY_VALUE_HEADS
    scale = 1.0 / math.sqrt(HEAD_SIZE)
    grouped_heads = query_matrix.astype(jnp.float32).reshape(count_of_rows, KEY_VALUE_HEADS, group_width, HEAD_SIZE)
    scores = jnp.einsum('tgjd,kgd->tgjk', grouped_heads, key_rows.astype(jnp.float32), precision=lax.Precision.HIGHEST) * scale
    allowed = (query_docs[:, None] == key_docs[None, :]) & (key_spots[None, :] <= query_spots[:, None])
    inside = allowed[:, None, None, :]
    masked = jnp.where(inside, scores, LOW_SCORE)
    row_peak = lax.optimization_barrier(jnp.max(masked, axis=-1, keepdims=True))
    weight = jnp.where(inside, jnp.exp(masked - row_peak), 0.0)
    row_total = lax.optimization_barrier(jnp.sum(weight, axis=-1))
    rounded = lax.optimization_barrier(weight.astype(jnp.bfloat16)).astype(jnp.float32)
    mixture = jnp.einsum('tgjk,kgd->tgjd', rounded, value_rows.astype(jnp.float32), precision=lax.Precision.HIGHEST)
    return (mixture / row_total[..., None]).reshape(count_of_rows, QUERY_HEADS * HEAD_SIZE).astype(jnp.bfloat16)

def reference(queries, key_heads, section_values, block_docs):
    token_docs = jnp.repeat(block_docs, BLK)
    window = SPAN * TOK_DEV
    positions = jnp.arange(PACKED_TOKENS, dtype=jnp.int32)
    layers = []
    for section_index in range(RELAY_SECTIONS):

        def one_block(block_index):
            first_row = (block_index * TOK_DEV).astype(jnp.int32)
            key_first = jnp.clip(first_row - (SPAN - 1) * TOK_DEV, 0, PACKED_TOKENS - window).astype(jnp.int32)
            query_matrix = lax.dynamic_slice_in_dim(queries[section_index], first_row, TOK_DEV, 0)
            key_rows = lax.dynamic_slice_in_dim(key_heads[section_index], key_first, window, 0)
            value_rows = lax.dynamic_slice_in_dim(section_values[section_index], key_first, window, 0)
            query_docs = lax.dynamic_slice_in_dim(token_docs, first_row, TOK_DEV, 0)
            key_docs = lax.dynamic_slice_in_dim(token_docs, key_first, window, 0)
            query_spots = lax.dynamic_slice_in_dim(positions, first_row, TOK_DEV, 0)
            key_spots = lax.dynamic_slice_in_dim(positions, key_first, window, 0)
            return block_attention(query_matrix, key_rows, value_rows, query_docs, key_docs, query_spots, key_spots)
        blocks = lax.map(one_block, jnp.arange(N_CTX, dtype=jnp.int32))
        layers.append(blocks.reshape(PACKED_TOKENS, QUERY_HEADS * HEAD_SIZE))
    attention = jnp.stack(layers)
    return jnp.roll(attention, 1, axis=0)
```

```python
import functools
import math

import jax
import jax.numpy as jnp
from jax import lax
from jax.experimental import pallas as pl
from jax.experimental.pallas import tpu as pltpu
from jax.sharding import PartitionSpec as P

MESH = pl.DeviceIdType.MESH
MIB = 1 << 20
BLK = 128
TOK = 256
D = 128
GROUPS = 4
WIDTH = 8
HEADS = GROUPS * WIDTH
KEYS = 15 * BLK
TILE = 512
PER_TILE = TILE // BLK
CHUNK = 256
NY = 4
NZ = 8
NX = 4
EARLY = GROUPS - 1
LOW_SCORE = -1e30
SCALE = math.log2(math.e) / math.sqrt(D)


def score_tile(q, km, scores, peaks, causal):
    peak = None
    for c in range(0, KEYS, CHUNK):
        w = min(CHUNK, KEYS - c)
        s = lax.dot_general(
            q, km[c : c + w], (((1,), (1,)), ((), ())), preferred_element_type=jnp.float32
        )
        if c + w == KEYS:
            last = jnp.where(causal, s[:, w - BLK :], LOW_SCORE)
            s = last if w == BLK else jnp.concatenate([s[:, : w - BLK], last], axis=1)
        scores[:, c : c + w] = s
        for b in range(0, w, BLK):
            part = s[:, b : b + BLK]
            peak = part if peak is None else jnp.maximum(peak, part)
    peaks[...] = peak


def mix_tile(scores, peaks, weights, va):
    peak = jnp.max(peaks[...], axis=1, keepdims=True)
    for c in range(0, KEYS, CHUNK):
        w = min(CHUNK, KEYS - c)
        weights[:, c : c + w] = jnp.exp2((scores[:, c : c + w] - peak) * SCALE).astype(jnp.bfloat16)
    mixed = jnp.dot(weights[...], va[...], preferred_element_type=jnp.float32)
    return mixed[:, :D] / mixed[:, D:]


def kernel(
    docs, q_hbm, k_hbm, v_hbm, out_hbm,
    q_in, k_in, v_in, wide, heads, first, kv, km, va,
    scores_a, scores_b, peaks_a, peaks_b, weights_a, weights_b, done,
    in_sem, g_send, g_recv, e_send, e_recv, x_send, x_recv, l_sem,
):
    sec, ctx, tp = lax.axis_index("section"), lax.axis_index("ctx"), lax.axis_index("tp")
    z, y = ctx // NY, ctx % NY
    after, before = (sec + 1) % NX, (sec + NX - 1) % NX

    def at(s, zz, yy):
        return (s, zz * NY + yy, tp)

    load_k = pltpu.make_async_copy(k_hbm, k_in, in_sem.at[0])
    load_v = pltpu.make_async_copy(v_hbm, v_in, in_sem.at[1])
    load_q = pltpu.make_async_copy(q_hbm, q_in, in_sem.at[2])
    load_k.start()
    load_v.start()
    load_q.start()

    barrier = pltpu.get_barrier_semaphore()
    peers = [at(after, z, y), at(before, z, y)]
    peers += [at(sec, z, (y + i) % NY) for i in range(1, NY)]
    peers += [at(sec, (z + i) % NZ, y) for i in (1, 2, NZ - 2, NZ - 1)]
    for peer in peers:
        pl.semaphore_signal(barrier, inc=1, device_id=peer, device_id_type=MESH)

    for i, (load, source) in enumerate(((load_k, k_in), (load_v, v_in))):
        load.wait()
        rows = TOK * GROUPS
        wide[:rows] = source[...].astype(jnp.float32)
        for g in range(GROUPS):
            part = wide[pl.ds(g, TOK, stride=GROUPS), :].astype(jnp.bfloat16)
            if g == EARLY:
                first[i] = part
            else:
                kv[g, 0, i] = part

    pl.semaphore_wait(barrier, len(peers))

    def remote(src, dst, ssem, rsem, peer):
        return pltpu.make_async_remote_copy(
            src_ref=src, dst_ref=dst, send_sem=ssem, recv_sem=rsem,
            device_id=peer, device_id_type=MESH,
        )

    def block_copy(g, src_slot, dst_slot, send_slot, peer):
        return remote(
            kv.at[g, src_slot], kv.at[g, dst_slot], g_send.at[g, send_slot],
            g_recv.at[g, dst_slot], peer,
        )

    def to_z(g, steps):
        return block_copy(g, 0, 4 * steps, steps - 1, at(sec, (z + steps) % NZ, y))

    def to_y(g, src_slot, dst_slot, dy):
        return block_copy(g, src_slot, dst_slot, dst_slot + (1 if dst_slot < 4 else 0), at(sec, z, (y + dy) % NY))

    def z_pairs():
        return ((1, z < NZ - 1), (2, jnp.logical_and(z < NZ - 2, y > 0)))

    def y_own():
        return [(0, dy, dy, y + dy < NY) for dy in range(1, NY)]

    def y_near():
        near = [(4, 4 + dy, dy, jnp.logical_and(z >= 1, y + dy < NY)) for dy in range(1, NY)]
        return near + [(4, dy, dy, jnp.logical_and(z >= 1, y + dy >= NY)) for dy in range(1, NY)]

    def y_far():
        return [(8, 4 + dy, dy, jnp.logical_and(z >= 2, y + dy >= NY)) for dy in range(1, NY)]

    def arrived(g, slot, cond):
        @pl.when(cond)
        def _():
            block_copy(g, slot, slot, 0, at(after, z, y)).wait_recv()

    def direct(g):
        for steps, cond in z_pairs():
            @pl.when(cond)
            def _():
                to_z(g, steps).start()
        for src, dst, dy, cond in y_own():
            @pl.when(cond)
            def _():
                to_y(g, src, dst, dy).start()

    def relay(g):
        arrived(g, 4, z >= 1)
        for src, dst, dy, cond in y_near():
            @pl.when(cond)
            def _():
                to_y(g, src, dst, dy).start()
        arrived(g, 8, jnp.logical_and(z >= 2, y > 0))
        for src, dst, dy, cond in y_far():
            @pl.when(cond)
            def _():
                to_y(g, src, dst, dy).start()

    early_kv = remote(first, kv.at[EARLY, 0], e_send.at[0], e_recv.at[0], at(after, z, y))
    early_q = remote(
        heads.at[pl.ds(EARLY * WIDTH, WIDTH)], heads.at[pl.ds(HEADS, WIDTH)],
        e_send.at[1], e_recv.at[1], at(after, z, y),
    )

    direct(0)
    early_kv.start()
    load_q.wait()
    wide[...] = q_in[...].astype(jnp.float32)
    for h in [*range(EARLY * WIDTH, HEADS), *range(EARLY * WIDTH)]:
        heads[h] = wide[pl.ds(h, TOK, stride=HEADS), :].astype(jnp.bfloat16)
        if h == HEADS - 1:
            early_q.start()
            direct(1)
    relay(0)

    row = lax.broadcasted_iota(jnp.int32, (BLK, BLK), 0)
    col = lax.broadcasted_iota(jnp.int32, (BLK, BLK), 1)
    causal = jnp.concatenate([row >= col] * PER_TILE, axis=0)

    def out_copy(g, r, peer):
        src = done.at[g, pl.ds(r * BLK, BLK)]
        dst = out_hbm.at[pl.ds(r * BLK, BLK), pl.ds(pl.multiple_of(g * WIDTH * D, WIDTH * D), WIDTH * D)]
        if peer is None:
            return pltpu.make_async_copy(src, dst, l_sem.at[r])
        return remote(src, dst, x_send.at[g, r], x_recv.at[g, r], peer)

    def group(g, carry):
        @pl.when(g == 1)
        def _():
            early_kv.wait_recv()

        @pl.when(g < GROUPS - 2)
        def _():
            direct(g + 2)

        @pl.when(g < GROUPS - 1)
        def _():
            relay(g + 1)

        for slot in (1, 2, 3, 5, 6, 7):
            arrived(g, slot, ctx >= slot)

        for r in range(2):
            mine = docs[2 * ctx + r]
            spare = jnp.broadcast_to(kv[g, 0, 0, r * BLK : r * BLK + 16][:1], (BLK, D))
            for b in range(15):
                place = r + b
                slot, half = 7 - place // 2, place % 2
                rows = slice(half * BLK, half * BLK + BLK)
                to = slice(b * BLK, b * BLK + BLK)
                key, value = kv[g, slot, 0, rows], kv[g, slot, 1, rows]
                if b == 14:
                    km[r, to] = key
                    va[r, to, :D] = value
                    va[r, to, D:] = jnp.ones((BLK, D), jnp.bfloat16)
                else:
                    block = 2 * ctx + r - 14 + b
                    ok = jnp.logical_and(block >= 0, docs[jnp.maximum(block, 0)] == mine)
                    ok = jnp.full((BLK, D), ok.astype(jnp.int32)) > 0
                    km[r, to] = jnp.where(ok, key, spare)
                    va[r, to, :D] = jnp.where(ok, value, jnp.zeros_like(value))
                    va[r, to, D:] = jnp.where(ok, 1.0, 0.0).astype(jnp.bfloat16)

        @pl.when(g == EARLY)
        def _():
            early_q.wait_recv()

        base = g * WIDTH + (g // EARLY) * WIDTH

        def queries(r, n):
            return heads[pl.ds(base + n * PER_TILE, PER_TILE), r * BLK : r * BLK + BLK].reshape(TILE, D)

        def put(r, n, mixed):
            for i in range(PER_TILE):
                h = n * PER_TILE + i
                done[g, r * BLK : r * BLK + BLK, h * D : h * D + D] = mixed[
                    i * BLK : i * BLK + BLK
                ].astype(jnp.bfloat16)

        sides = ((scores_a, peaks_a, weights_a), (scores_b, peaks_b, weights_b))
        tiles = [(r, n) for r in range(2) for n in range(WIDTH // PER_TILE)]
        score_tile(queries(0, 0), km.at[0], scores_a, peaks_a, causal)
        for i, (r, n) in enumerate(tiles):
            if i + 1 < len(tiles):
                r1, n1 = tiles[i + 1]
                scores, peaks, _ = sides[(i + 1) % 2]
                score_tile(queries(r1, n1), km.at[r1], scores, peaks, causal)
            scores, peaks, weights = sides[i % 2]
            put(r, n, mix_tile(scores, peaks, weights, va.at[r]))
            if n == WIDTH // PER_TILE - 1:
                @pl.when(g < EARLY)
                def _():
                    out_copy(g, r, at(after, z, y)).start()

                @pl.when(g == EARLY)
                def _():
                    out_copy(g, r, None).start()
        return carry

    lax.fori_loop(0, GROUPS, group, 0)

    early_kv.wait_send()
    early_q.wait_send()
    for r in range(2):
        out_copy(EARLY, r, None).wait()

    def finish(g, carry):
        for steps, cond in z_pairs():
            @pl.when(cond)
            def _():
                to_z(g, steps).wait_send()
        for src, dst, dy, cond in y_own() + y_near() + y_far():
            @pl.when(cond)
            def _():
                to_y(g, src, dst, dy).wait_send()

        @pl.when(g < EARLY)
        def _():
            for r in range(2):
                out_copy(g, r, at(after, z, y)).wait()
        return carry

    lax.fori_loop(0, GROUPS, finish, 0)


def local(queries, key_heads, section_values, block_docs):
    bf16, f32 = jnp.bfloat16, jnp.float32
    anywhere = pl.BlockSpec(memory_space=pl.ANY)
    out = pl.pallas_call(
        kernel,
        out_shape=jax.ShapeDtypeStruct((TOK, HEADS * D), bf16),
        in_specs=[pl.BlockSpec(memory_space=pltpu.SMEM), anywhere, anywhere, anywhere],
        out_specs=anywhere,
        scratch_shapes=[
            pltpu.VMEM((TOK * HEADS, D), bf16),
            pltpu.VMEM((TOK * GROUPS, D), bf16),
            pltpu.VMEM((TOK * GROUPS, D), bf16),
            pltpu.VMEM((TOK * HEADS, D), f32),
            pltpu.VMEM((HEADS + WIDTH, TOK, D), bf16),
            pltpu.VMEM((2, TOK, D), bf16),
            pltpu.VMEM((GROUPS, 9, 2, TOK, D), bf16),
            pltpu.VMEM((2, KEYS, D), bf16),
            pltpu.VMEM((2, KEYS, 2 * D), bf16),
            pltpu.VMEM((TILE, KEYS), f32),
            pltpu.VMEM((TILE, KEYS), f32),
            pltpu.VMEM((TILE, BLK), f32),
            pltpu.VMEM((TILE, BLK), f32),
            pltpu.VMEM((TILE, KEYS), bf16),
            pltpu.VMEM((TILE, KEYS), bf16),
            pltpu.VMEM((GROUPS, TOK, WIDTH * D), bf16),
            pltpu.SemaphoreType.DMA((3,)),
            pltpu.SemaphoreType.DMA((GROUPS, 9)),
            pltpu.SemaphoreType.DMA((GROUPS, 9)),
            pltpu.SemaphoreType.DMA((2,)),
            pltpu.SemaphoreType.DMA((2,)),
            pltpu.SemaphoreType.DMA((GROUPS, 2)),
            pltpu.SemaphoreType.DMA((GROUPS, 2)),
            pltpu.SemaphoreType.DMA((2,)),
        ],
        compiler_params=pltpu.CompilerParams(
            collective_id=0, has_side_effects=True, vmem_limit_bytes=56 * MIB
        ),
    )(
        block_docs,
        queries.reshape(TOK * HEADS, D),
        key_heads.reshape(TOK * GROUPS, D),
        section_values.reshape(TOK * GROUPS, D),
    )
    return out[None]


def solution(mesh):
    specs = P("section", "ctx", "tp", None)
    return jax.shard_map(
        local,
        mesh=mesh,
        in_specs=(specs, specs, specs, P()),
        out_specs=P("section", "ctx", "tp"),
        check_vma=False,
    )
```

```python
import functools
import math

import jax
import jax.numpy as jnp
from jax import lax
from jax.experimental import pallas as pl
from jax.experimental.pallas import tpu as pltpu
from jax.sharding import PartitionSpec as P

MESH = pl.DeviceIdType.MESH
MIB = 1 << 20
BLK = 128
TOK = 256
D = 128
GROUPS = 4
WIDTH = 8
HEADS = GROUPS * WIDTH
NEAR = 11 * BLK
FAR = 4 * BLK
TILE = 512
PER_TILE = TILE // BLK
CHUNK = 256
NY = 4
NZ = 8
NX = 4
EARLY = 2
LONG = 4
SHORT = WIDTH - LONG
LOW_SCORE = -1e30
SCALE = math.log2(math.e) / math.sqrt(D)


def score_tile(q, km, scores, peaks, causal):
    keys, peak = km.shape[0], None
    for c in range(0, keys, CHUNK):
        w = min(CHUNK, keys - c)
        s = lax.dot_general(
            q, km[c : c + w], (((1,), (1,)), ((), ())), preferred_element_type=jnp.float32
        )
        if causal is not None and c + w == keys:
            last = jnp.where(causal, s[:, w - BLK :], LOW_SCORE)
            s = last if w == BLK else jnp.concatenate([s[:, : w - BLK], last], axis=1)
        scores[:, c : c + w] = s
        for b in range(0, w, BLK):
            part = s[:, b : b + BLK]
            peak = part if peak is None else jnp.maximum(peak, part)
    peaks[...] = peak


def mix_tile(scores, peak, weights, va):
    keys = va.shape[0]
    for c in range(0, keys, CHUNK):
        w = min(CHUNK, keys - c)
        weights[:, c : c + w] = jnp.exp2((scores[:, c : c + w] - peak) * SCALE).astype(jnp.bfloat16)
    return jnp.dot(weights[:, :keys], va[...], preferred_element_type=jnp.float32)


def kernel(
    docs, q_hbm, k_hbm, v_hbm, out_hbm,
    q_in, k_in, v_in, wide, heads, first, kv, km_near, va_near, km_far, va_far,
    scores_a, scores_b, peaks_a, peaks_b, weights_a, weights_b, kept_mix, kept_peak, done, hop_q,
    in_sem, g_send, g_recv, r_send, r_recv, k_send, k_recv, q_send, q_recv, hq_send, hq_recv,
    x_send, x_recv, l_sem,
):
    sec, ctx, tp = lax.axis_index("section"), lax.axis_index("ctx"), lax.axis_index("tp")
    z, y = ctx // NY, ctx % NY
    after, before = (sec + 1) % NX, (sec + NX - 1) % NX

    def at(s, zz, yy):
        return (s, zz * NY + yy, tp)

    load_k = pltpu.make_async_copy(k_hbm, k_in, in_sem.at[0])
    load_v = pltpu.make_async_copy(v_hbm, v_in, in_sem.at[1])
    load_q = pltpu.make_async_copy(q_hbm, q_in, in_sem.at[2])
    load_k.start()
    load_v.start()
    load_q.start()

    barrier = pltpu.get_barrier_semaphore()
    peers = [at(after, z, y), at(before, z, y)]
    peers += [at(sec, z, (y + i) % NY) for i in (1, NY - 1)]
    peers += [at(sec, (z + i) % NZ, y) for i in (1, NZ - 1)]
    for peer in peers:
        pl.semaphore_signal(barrier, inc=1, device_id=peer, device_id_type=MESH)

    for i, (load, source) in enumerate(((load_k, k_in), (load_v, v_in))):
        load.wait()
        rows = TOK * GROUPS
        wide[:rows] = source[...].astype(jnp.float32)
        for g in range(GROUPS):
            part = wide[pl.ds(g, TOK, stride=GROUPS), :].astype(jnp.bfloat16)
            if g < EARLY:
                kv[g, 0, i] = part
            else:
                first[g - EARLY, i] = part

    pl.semaphore_wait(barrier, len(peers))

    def remote(src, dst, ssem, rsem, peer):
        return pltpu.make_async_remote_copy(
            src_ref=src, dst_ref=dst, send_sem=ssem, recv_sem=rsem,
            device_id=peer, device_id_type=MESH,
        )

    def block_copy(g, src_slot, dst_slot, send_slot, peer):
        return remote(
            kv.at[g, src_slot], kv.at[g, dst_slot], g_send.at[g, send_slot],
            g_recv.at[g, dst_slot], peer,
        )

    def to_z(g, src_slot):
        return block_copy(g, src_slot, src_slot + 4, src_slot // 4, at(sec, (z + 1) % NZ, y))

    def to_y(g, src_slot, dst_slot, dy):
        return block_copy(g, src_slot, dst_slot, dst_slot + (1 if dst_slot < 4 else 0), at(sec, z, (y + dy) % NY))

    def z_pairs():
        onward = jnp.logical_and(z >= 1, jnp.logical_and(z < NZ - 1, y > 0))
        return ((0, z < NZ - 1), (4, onward))

    def y_own():
        return [(0, dy, dy, y + dy < NY) for dy in (1, NY - 1)]

    def y_near():
        near = [(4, 4 + dy, dy, jnp.logical_and(z >= 1, y + dy < NY)) for dy in (1, NY - 1)]
        return near + [(4, dy, dy, jnp.logical_and(z >= 1, y + dy >= NY)) for dy in (1, NY - 1)]

    def y_far():
        return [(8, 4 + dy, dy, jnp.logical_and(z >= 2, y + dy >= NY)) for dy in (1, NY - 1)]

    def arrived(g, slot, cond):
        @pl.when(cond)
        def _():
            block_copy(g, slot, slot, 0, at(after, z, y)).wait_recv()

    def send_z(g, which):
        src, cond = z_pairs()[which]

        @pl.when(cond)
        def _():
            to_z(g, src).start()

    def send_y(g, which):
        for src, dst, dy, cond in which:
            @pl.when(cond)
            def _():
                to_y(g, src, dst, dy).start()

    def send_own(g):
        send_y(g, y_own())

    def send_near(g):
        arrived(g, 4, z >= 1)
        send_z(g, 1)
        send_y(g, y_near())

    def send_far(g):
        arrived(g, 8, jnp.logical_and(z >= 2, y > 0))
        send_y(g, y_far())

    passes = (
        (0, 0, 5, 6, 1, 2), (0, 0, 1, 2, 1, 1), (0, 0, 3, 6, -1, 1), (0, 1, 3, 6, -1, 1),
        (1, 0, 1, 2, 1, 0), (1, 0, 7, 6, -1, 2), (1, 1, 7, 6, -1, 2), (1, 0, 5, 6, 1, 1),
        (2, 0, 1, 2, 1, 0), (2, 1, 1, 2, 1, 0), (2, 1, 7, 6, -1, 2), (2, 1, 3, 2, -1, 1),
        (3, 1, 3, 2, -1, 0), (3, 1, 7, 6, -1, 1), (3, 0, 5, 2, 1, 1), (3, 1, 5, 2, 1, 1),
    )

    def pass_copy(g, part, here, there, dy):
        return remote(
            kv.at[g, here, part], kv.at[g, there, part], r_send.at[g, there // 4, part],
            r_recv.at[g, there // 4, part], at(sec, z, (y + NY + dy) % NY),
        )

    def each_pass(g, act):
        for i in range(4):
            for who, part, here, there, dy, least in passes[i::4]:
                @pl.when(jnp.logical_and(y == who, z >= least))
                def _():
                    act(pass_copy(g, part, here, there, dy))

    def relay_again(g):
        for slot in (1, 3, 5, 7):
            arrived(g, slot, ctx >= slot)
        each_pass(g, lambda copy: copy.start())

    def gathered(g):
        for slot in (2, 6):
            @pl.when(ctx >= slot)
            def _():
                for part in range(2):
                    pass_copy(g, part, slot, slot, 1).wait_recv()

    def early_kv(g):
        return remote(
            first.at[g - EARLY], kv.at[g, 0], k_send.at[g - EARLY], k_recv.at[g - EARLY],
            at(after, z, y),
        )

    moved = EARLY * WIDTH

    def early_q(g):
        return remote(
            heads.at[pl.ds(g * WIDTH, SHORT)], heads.at[pl.ds(g * WIDTH + moved, SHORT)],
            q_send.at[g - EARLY], q_recv.at[g - EARLY], at(after, z, y),
        )

    def long_q(g, step):
        i, own = g - EARLY, g * WIDTH + SHORT
        src = heads.at[pl.ds(own, LONG)] if step == 0 else hop_q.at[i, step - 1]
        dst = heads.at[pl.ds(own + moved, LONG)] if step == 2 else hop_q.at[i, step]
        return remote(src, dst, hq_send.at[i, step], hq_recv.at[i, step], at(before, z, y))

    def pass_q(g, step):
        long_q(g, step - 1).wait_recv()
        long_q(g, step).start()

    early = range(EARLY, GROUPS)
    send_z(0, 0)
    send_own(0)
    send_z(1, 0)
    for g in early:
        early_kv(g).start()
    load_q.wait()
    wide[...] = q_in[...].astype(jnp.float32)
    for h in [*range(moved, HEADS), *range(moved)]:
        heads[h] = wide[pl.ds(h, TOK, stride=HEADS), :].astype(jnp.bfloat16)
        if h >= moved and (h + 1) % WIDTH == 0:
            early_q(h // WIDTH).start()
            long_q(h // WIDTH, 0).start()
    send_near(0)
    send_own(1)
    send_far(0)
    early_kv(2).wait_recv()
    send_z(2, 0)
    early_kv(3).wait_recv()
    send_z(3, 0)
    pass_q(2, 1)

    row = lax.broadcasted_iota(jnp.int32, (BLK, BLK), 0)
    col = lax.broadcasted_iota(jnp.int32, (BLK, BLK), 1)
    causal = jnp.concatenate([row >= col] * PER_TILE, axis=0)

    def out_copy(g, r, peer):
        src = done.at[g, pl.ds(r * BLK, BLK)]
        dst = out_hbm.at[pl.ds(r * BLK, BLK), pl.ds(pl.multiple_of(g * WIDTH * D, WIDTH * D), WIDTH * D)]
        if peer is None:
            return pltpu.make_async_copy(src, dst, l_sem.at[g, r])
        return remote(src, dst, x_send.at[g, r], x_recv.at[g, r], peer)

    def fill(g, r, blocks, km, va):
        mine = docs[2 * ctx + r]
        spare = jnp.broadcast_to(kv[g, 0, 0, r * BLK : r * BLK + 16][:1], (BLK, D))
        for b, (slot, half) in enumerate(blocks):
            rows = slice(half * BLK, half * BLK + BLK)
            to = slice(b * BLK, b * BLK + BLK)
            key, value = kv[g, slot, 0, rows], kv[g, slot, 1, rows]
            if slot == 0 and half == r:
                km[r, to] = key
                va[r, to, :D] = value
                va[r, to, D:] = jnp.ones((BLK, D), jnp.bfloat16)
            else:
                block = 2 * (ctx - slot) + half
                ok = jnp.logical_and(block >= 0, docs[jnp.maximum(block, 0)] == mine)
                ok = jnp.full((BLK, D), ok.astype(jnp.int32)) > 0
                km[r, to] = jnp.where(ok, key, spare)
                va[r, to, :D] = jnp.where(ok, value, jnp.zeros_like(value))
                va[r, to, D:] = jnp.where(ok, 1.0, 0.0).astype(jnp.bfloat16)

    near_blocks = [(slot, half) for slot in (1, 3, 4, 5) for half in range(2)]
    near_of = (
        near_blocks + [(7, 0), (7, 1), (0, 0)],
        near_blocks + [(7, 1), (0, 0), (0, 1)],
    )
    far_blocks = [(slot, half) for slot in (2, 6) for half in range(2)]
    sides = ((scores_a, peaks_a, weights_a), (scores_b, peaks_b, weights_b))
    tiles = [(r, n) for r in range(2) for n in range(WIDTH // PER_TILE)]

    def group(g, carry):
        for slot in (1, 3, 5, 7):
            arrived(g, slot, ctx >= slot)
        each_pass(g, lambda copy: copy.start())

        @pl.when(g < GROUPS - 1)
        def _():
            send_near(g + 1)

        @pl.when(g < GROUPS - 2)
        def _():
            send_own(g + 2)

        @pl.when(g == 1)
        def _():
            pass_q(2, 2)

        @pl.when(g == 2)
        def _():
            pass_q(3, 2)

        for r in range(2):
            fill(g, r, near_of[r], km_near, va_near)

        @pl.when(g == EARLY)
        def _():
            early_q(EARLY).wait_recv()
            long_q(EARLY, 2).wait_recv()

        @pl.when(g == EARLY + 1)
        def _():
            early_q(EARLY + 1).wait_recv()
            long_q(EARLY + 1, 2).wait_recv()

        base = g * WIDTH + (g // EARLY) * moved

        def queries(r, n):
            return heads[pl.ds(base + n * PER_TILE, PER_TILE), r * BLK : r * BLK + BLK].reshape(TILE, D)

        def score(i, km, mask):
            r, n = tiles[i]
            scores, peaks, _ = sides[i % 2]
            score_tile(queries(r, n), km.at[r], scores, peaks, mask)

        score(0, km_near, causal)
        for i, (r, n) in enumerate(tiles):
            if i + 1 < len(tiles):
                score(i + 1, km_near, causal)
            scores, peaks, weights = sides[i % 2]
            peak = jnp.max(peaks[...], axis=1, keepdims=True)
            kept_peak[i] = jnp.broadcast_to(peak, (TILE, D))
            kept_mix[i] = mix_tile(scores, peak, weights, va_near.at[r])
            if i == 1:
                @pl.when(g < GROUPS - 1)
                def _():
                    send_far(g + 1)

                @pl.when(g == 0)
                def _():
                    pass_q(3, 1)

        gathered(g)
        for r in range(2):
            fill(g, r, far_blocks, km_far, va_far)

        score(0, km_far, None)
        for i, (r, n) in enumerate(tiles):
            if i + 1 < len(tiles):
                score(i + 1, km_far, None)
            scores, peaks, weights = sides[i % 2]
            old = kept_peak[i][:, :1]
            peak = jnp.maximum(old, jnp.max(peaks[...], axis=1, keepdims=True))
            mixed = mix_tile(scores, peak, weights, va_far.at[r])
            mixed = mixed + kept_mix[i] * jnp.exp2((old - peak) * SCALE)
            mixed = (mixed[:, :D] / mixed[:, D:]).astype(jnp.bfloat16)
            for j in range(PER_TILE):
                h = n * PER_TILE + j
                done[g, r * BLK : r * BLK + BLK, h * D : h * D + D] = mixed[j * BLK : j * BLK + BLK]
            if n == WIDTH // PER_TILE - 1:
                @pl.when(g < EARLY)
                def _():
                    out_copy(g, r, at(after, z, y)).start()

                @pl.when(g >= EARLY)
                def _():
                    out_copy(g, r, None).start()
        return carry

    lax.fori_loop(0, GROUPS, group, 0)

    for g in early:
        early_kv(g).wait_send()
        early_q(g).wait_send()
        for step in range(3):
            long_q(g, step).wait_send()
        for r in range(2):
            out_copy(g, r, None).wait()
    for g in range(EARLY):
        for r in range(2):
            out_copy(g, r, at(after, z, y)).wait()

    def finish(g, carry):
        for src, cond in z_pairs():
            @pl.when(cond)
            def _():
                to_z(g, src).wait_send()
        for src, dst, dy, cond in y_own() + y_near() + y_far():
            @pl.when(cond)
            def _():
                to_y(g, src, dst, dy).wait_send()
        each_pass(g, lambda copy: copy.wait_send())
        return carry

    lax.fori_loop(0, GROUPS, finish, 0)


def local(queries, key_heads, section_values, block_docs):
    bf16, f32 = jnp.bfloat16, jnp.float32
    anywhere = pl.BlockSpec(memory_space=pl.ANY)
    late = GROUPS - EARLY
    dma = pltpu.SemaphoreType.DMA
    out = pl.pallas_call(
        kernel,
        out_shape=jax.ShapeDtypeStruct((TOK, HEADS * D), bf16),
        in_specs=[pl.BlockSpec(memory_space=pltpu.SMEM), anywhere, anywhere, anywhere],
        out_specs=anywhere,
        scratch_shapes=[
            pltpu.VMEM((TOK * HEADS, D), bf16),
            pltpu.VMEM((TOK * GROUPS, D), bf16),
            pltpu.VMEM((TOK * GROUPS, D), bf16),
            pltpu.VMEM((TOK * HEADS, D), f32),
            pltpu.VMEM((HEADS + late * WIDTH, TOK, D), bf16),
            pltpu.VMEM((late, 2, TOK, D), bf16),
            pltpu.VMEM((GROUPS, 9, 2, TOK, D), bf16),
            pltpu.VMEM((2, NEAR, D), bf16),
            pltpu.VMEM((2, NEAR, 2 * D), bf16),
            pltpu.VMEM((2, FAR, D), bf16),
            pltpu.VMEM((2, FAR, 2 * D), bf16),
            pltpu.VMEM((TILE, NEAR), f32),
            pltpu.VMEM((TILE, NEAR), f32),
            pltpu.VMEM((TILE, BLK), f32),
            pltpu.VMEM((TILE, BLK), f32),
            pltpu.VMEM((TILE, NEAR), bf16),
            pltpu.VMEM((TILE, NEAR), bf16),
            pltpu.VMEM((4, TILE, 2 * D), f32),
            pltpu.VMEM((4, TILE, D), f32),
            pltpu.VMEM((GROUPS, TOK, WIDTH * D), bf16),
            pltpu.VMEM((late, 2, LONG, TOK, D), bf16),
            dma((3,)),
            dma((GROUPS, 9)),
            dma((GROUPS, 9)),
            dma((GROUPS, 2, 2)),
            dma((GROUPS, 2, 2)),
            dma((late,)),
            dma((late,)),
            dma((late,)),
            dma((late,)),
            dma((late, 3)),
            dma((late, 3)),
            dma((EARLY, 2)),
            dma((EARLY, 2)),
            dma((GROUPS, 2)),
        ],
        compiler_params=pltpu.CompilerParams(
            collective_id=0, has_side_effects=True, vmem_limit_bytes=56 * MIB
        ),
    )(
        block_docs,
        queries.reshape(TOK * HEADS, D),
        key_heads.reshape(TOK * GROUPS, D),
        section_values.reshape(TOK * GROUPS, D),
    )
    return out[None]


def solution(mesh):
    specs = P("section", "ctx", "tp", None)
    return jax.shard_map(
        local,
        mesh=mesh,
        in_specs=(specs, specs, specs, P()),
        out_specs=P("section", "ctx", "tp"),
        check_vma=False,
    )
```

```python
import functools
import math

import jax
import jax.numpy as jnp
from jax import lax
from jax.experimental import pallas as pl
from jax.experimental.pallas import tpu as pltpu
from jax.sharding import PartitionSpec as P

MESH = pl.DeviceIdType.MESH
MIB = 1 << 20
BLK = 128
TOK = 256
D = 128
GROUPS = 4
WIDTH = 8
HEADS = GROUPS * WIDTH
NEAR = 11 * BLK
FAR = 4 * BLK
TILE = 1024
PER_TILE = TILE // BLK
CHUNK = 256
NY = 4
NZ = 8
NX = 4
EARLY = 2
LONG = 2
SHORT = WIDTH - LONG
LOW_SCORE = -1e30
SCALE = math.log2(math.e) / math.sqrt(D)


def score_tile(q, pieces, scores, peaks, causal):
    peak, c = None, 0
    for i, (keys, added) in enumerate(pieces):
        s = lax.dot_general(
            q, keys, (((1,), (1,)), ((), ())), preferred_element_type=jnp.float32
        )
        for b, bias in enumerate(added):
            part = s[:, b * BLK : b * BLK + BLK]
            if causal is not None and i + 1 == len(pieces) and b + 1 == len(added):
                part = jnp.where(causal, part, LOW_SCORE)
            else:
                part = part + bias
            scores[:, c : c + BLK] = part
            peak = part if peak is None else jnp.maximum(peak, part)
            c += BLK
    peaks[...] = peak


def mix_tile(scores, peaks, weights, va):
    keys = va.shape[0]
    for t in range(0, TILE, BLK):
        rows = slice(t, t + BLK)
        peak = peaks[rows]
        for c in range(0, keys, BLK):
            part = jnp.exp2((scores[rows, c : c + BLK] - peak) * SCALE)
            weights[rows, c : c + BLK] = part.astype(jnp.bfloat16)
    return jnp.dot(weights[:, :keys], va[...], preferred_element_type=jnp.float32)


def kernel(
    docs, q_hbm, k_hbm, v_hbm, out_hbm,
    q_in, k_in, v_in, wide, heads, first, kv, va_near, va_far,
    scores_a, scores_b, peaks_a, peaks_b, weights_a, weights_b, kept_mix, kept_peak, far_mix, done, hop_q, hop_o,
    in_sem, g_send, g_recv, r_send, r_recv, k_send, k_recv, q_send, q_recv, hq_send, hq_recv,
    ho_send, ho_recv, x_send, x_recv, l_sem,
):
    sec, ctx, tp = lax.axis_index("section"), lax.axis_index("ctx"), lax.axis_index("tp")
    z, y = ctx // NY, ctx % NY
    after, before = (sec + 1) % NX, (sec + NX - 1) % NX

    def at(s, zz, yy):
        return (s, zz * NY + yy, tp)

    load_k = pltpu.make_async_copy(k_hbm, k_in, in_sem.at[0])
    load_v = pltpu.make_async_copy(v_hbm, v_in, in_sem.at[1])
    load_q = pltpu.make_async_copy(q_hbm, q_in, in_sem.at[2])
    load_k.start()
    load_v.start()
    load_q.start()

    barrier = pltpu.get_barrier_semaphore()
    peers = [at(after, z, y), at(before, z, y)]
    peers += [at(sec, z, (y + i) % NY) for i in (1, NY - 1)]
    peers += [at(sec, (z + i) % NZ, y) for i in (1, NZ - 1)]
    for peer in peers:
        pl.semaphore_signal(barrier, inc=1, device_id=peer, device_id_type=MESH)

    for i, (load, source) in enumerate(((load_k, k_in), (load_v, v_in))):
        load.wait()
        rows = TOK * GROUPS
        wide[:rows] = source[...].astype(jnp.float32)
        for g in range(GROUPS):
            part = wide[pl.ds(g, TOK, stride=GROUPS), :].astype(jnp.bfloat16)
            if g < EARLY:
                kv[g, 0, i] = part
            else:
                first[g - EARLY, i] = part

    pl.semaphore_wait(barrier, len(peers))

    def remote(src, dst, ssem, rsem, peer):
        return pltpu.make_async_remote_copy(
            src_ref=src, dst_ref=dst, send_sem=ssem, recv_sem=rsem,
            device_id=peer, device_id_type=MESH,
        )

    def block_copy(g, src_slot, dst_slot, send_slot, peer):
        return remote(
            kv.at[g, src_slot], kv.at[g, dst_slot], g_send.at[g, send_slot],
            g_recv.at[g, dst_slot], peer,
        )

    def to_z(g, src_slot):
        return block_copy(g, src_slot, src_slot + 4, src_slot // 4, at(sec, (z + 1) % NZ, y))

    def to_y(g, src_slot, dst_slot, dy):
        return block_copy(g, src_slot, dst_slot, dst_slot + (1 if dst_slot < 4 else 0), at(sec, z, (y + dy) % NY))

    def z_pairs():
        onward = jnp.logical_and(z >= 1, jnp.logical_and(z < NZ - 1, y > 0))
        return ((0, z < NZ - 1), (4, onward))

    def y_own():
        return [(0, dy, dy, y + dy < NY) for dy in (1, NY - 1)]

    def y_near():
        near = [(4, 4 + dy, dy, jnp.logical_and(z >= 1, y + dy < NY)) for dy in (1, NY - 1)]
        return near + [(4, dy, dy, jnp.logical_and(z >= 1, y + dy >= NY)) for dy in (1, NY - 1)]

    def y_far():
        return [(8, 4 + dy, dy, jnp.logical_and(z >= 2, y + dy >= NY)) for dy in (1, NY - 1)]

    def arrived(g, slot, cond):
        @pl.when(cond)
        def _():
            block_copy(g, slot, slot, 0, at(after, z, y)).wait_recv()

    def send_z(g, which):
        src, cond = z_pairs()[which]

        @pl.when(cond)
        def _():
            to_z(g, src).start()

    def send_y(g, which):
        for src, dst, dy, cond in which:
            @pl.when(cond)
            def _():
                to_y(g, src, dst, dy).start()

    def send_own(g):
        send_y(g, y_own())

    def send_near(g):
        arrived(g, 4, z >= 1)
        send_z(g, 1)
        send_y(g, y_near())

    def send_far(g):
        arrived(g, 8, jnp.logical_and(z >= 2, y > 0))
        send_y(g, y_far())

    passes = (
        (0, 0, 5, 6, 1, 2), (0, 0, 1, 2, 1, 1), (0, 0, 3, 6, -1, 1), (0, 1, 3, 6, -1, 1),
        (1, 0, 1, 2, 1, 0), (1, 0, 7, 6, -1, 2), (1, 1, 7, 6, -1, 2), (1, 0, 5, 6, 1, 1),
        (2, 0, 1, 2, 1, 0), (2, 1, 1, 2, 1, 0), (2, 1, 7, 6, -1, 2), (2, 1, 3, 2, -1, 1),
        (3, 1, 3, 2, -1, 0), (3, 1, 7, 6, -1, 1), (3, 0, 5, 2, 1, 1), (3, 1, 5, 2, 1, 1),
    )

    def pass_copy(g, part, here, there, dy):
        return remote(
            kv.at[g, here, part], kv.at[g, there, part], r_send.at[g, there // 4, part],
            r_recv.at[g, there // 4, part], at(sec, z, (y + NY + dy) % NY),
        )

    def each_pass(g, act):
        for i in range(4):
            for who, part, here, there, dy, least in passes[i::4]:
                @pl.when(jnp.logical_and(y == who, z >= least))
                def _():
                    act(pass_copy(g, part, here, there, dy))

    def relay_again(g):
        for slot in (1, 3, 5, 7):
            arrived(g, slot, ctx >= slot)
        each_pass(g, lambda copy: copy.start())

    def gathered(g):
        for slot in (2, 6):
            @pl.when(ctx >= slot)
            def _():
                for part in range(2):
                    pass_copy(g, part, slot, slot, 1).wait_recv()

    def early_kv(g):
        return remote(
            first.at[g - EARLY], kv.at[g, 0], k_send.at[g - EARLY], k_recv.at[g - EARLY],
            at(after, z, y),
        )

    moved = EARLY * WIDTH

    def early_q(g):
        count = WIDTH if g == EARLY else SHORT
        return remote(
            heads.at[pl.ds(g * WIDTH, count)], heads.at[pl.ds(g * WIDTH + moved, count)],
            q_send.at[g - EARLY], q_recv.at[g - EARLY], at(after, z, y),
        )

    def long_q(step):
        own = (GROUPS - 1) * WIDTH + SHORT
        src = heads.at[pl.ds(own, LONG)] if step == 0 else hop_q.at[step - 1]
        dst = heads.at[pl.ds(own + moved, LONG)] if step == 2 else hop_q.at[step]
        return remote(src, dst, hq_send.at[step], hq_recv.at[step], at(before, z, y))

    def long_out(g, step):
        cols = pl.ds(SHORT * D, LONG * D)
        far_cols = pl.ds(pl.multiple_of(g * WIDTH * D + SHORT * D, LONG * D), LONG * D)
        src = done.at[g, :, cols] if step == 0 else hop_o.at[g, step - 1]
        dst = out_hbm.at[:, far_cols] if step == 2 else hop_o.at[g, step]
        return remote(src, dst, ho_send.at[g, step], ho_recv.at[g, step], at(before, z, y))

    def pass_q(step):
        long_q(step - 1).wait_recv()
        long_q(step).start()

    def pass_out(g, step):
        long_out(g, step - 1).wait_recv()
        long_out(g, step).start()

    early = range(EARLY, GROUPS)
    send_z(0, 0)
    send_own(0)
    send_z(1, 0)
    for g in early:
        early_kv(g).start()
    load_q.wait()
    wide[...] = q_in[...].astype(jnp.float32)
    for h in [*range(moved, HEADS), *range(moved)]:
        heads[h] = wide[pl.ds(h, TOK, stride=HEADS), :].astype(jnp.bfloat16)
        if h >= moved and (h + 1) % WIDTH == 0:
            early_q(h // WIDTH).start()
        if h == HEADS - 1:
            long_q(0).start()
    va_near[:, D:] = jnp.ones((NEAR + BLK, D), jnp.bfloat16)
    va_far[:, D:] = jnp.ones((FAR, D), jnp.bfloat16)
    for slot in range(1, 8):
        @pl.when(ctx < slot)
        def _():
            for g in range(GROUPS):
                kv[g, slot] = jnp.zeros((2, TOK, D), jnp.bfloat16)

    send_near(0)
    send_own(1)
    send_near(1)
    early_kv(2).wait_recv()
    send_z(2, 0)
    early_kv(3).wait_recv()
    send_z(3, 0)
    send_far(0)
    pass_q(1)
    send_far(1)

    row = lax.broadcasted_iota(jnp.int32, (BLK, BLK), 0)
    col = lax.broadcasted_iota(jnp.int32, (BLK, BLK), 1)
    causal = jnp.concatenate([row >= col] * PER_TILE, axis=0)

    def out_copy(g, r, peer):
        width = WIDTH * D if peer is None else SHORT * D
        src = done.at[g, pl.ds(r * BLK, BLK), pl.ds(0, width)]
        dst = out_hbm.at[pl.ds(r * BLK, BLK), pl.ds(pl.multiple_of(g * WIDTH * D, WIDTH * D), width)]
        if peer is None:
            return pltpu.make_async_copy(src, dst, l_sem.at[g, r])
        return remote(src, dst, x_send.at[g, r], x_recv.at[g, r], peer)

    near_slots, far_slots = (7, 1, 3, 4, 5, 0), (2, 6)

    def bring(g, slots, va):
        for i, slot in enumerate(slots):
            va[i * TOK : i * TOK + TOK, :D] = kv[g, slot, 1]

    def pieces_of(g, r, slots):
        mine = docs[2 * ctx + r]
        pieces = []
        for slot in slots:
            halves = (0,) if (slot, r) == (0, 0) else (1,) if (slot, r) == (7, 1) else (0, 1)
            keys = kv[g, slot, 0, halves[0] * BLK : halves[-1] * BLK + BLK]
            added = []
            for half in halves:
                block = 2 * (ctx - slot) + half
                ok = jnp.logical_and(block >= 0, docs[jnp.maximum(block, 0)] == mine)
                added.append(jnp.where(ok, 0.0, LOW_SCORE).astype(jnp.float32))
            pieces.append((keys, added))
        return pieces

    def va_of(r):
        return va_near.at[r * BLK : r * BLK + NEAR]

    sides = ((scores_a, peaks_a, weights_a), (scores_b, peaks_b, weights_b))

    def score(g, r, slots, mask):
        base = g * WIDTH + (g // EARLY) * moved
        q = heads[pl.ds(base, WIDTH), r * BLK : r * BLK + BLK].reshape(TILE, D)
        scores, peaks, _ = sides[r]
        score_tile(q, pieces_of(g, r, slots), scores, peaks, mask)

    def near_part(i, p):
        g = EARLY * p + i

        @pl.when(g == 2)
        def _():
            send_far(3)

        for slot in (1, 3, 5, 7):
            arrived(g, slot, ctx >= slot)
        each_pass(g, lambda copy: copy.start())

        @pl.when(g == 0)
        def _():
            send_near(2)
            send_own(2)
            pass_q(2)

        @pl.when(g == 2)
        def _():
            early_q(2).wait_recv()

        @pl.when(g == 3)
        def _():
            pass_out(1, 1)
            early_q(3).wait_recv()
            long_q(2).wait_recv()

        bring(g, near_slots, va_near)

        score(g, 0, near_slots, causal)
        for r in range(2):
            if r == 0:
                score(g, 1, near_slots, causal)
            scores, peaks, weights = sides[r]
            for t in range(0, TILE, BLK):
                rows = slice(t, t + BLK)
                peak = jnp.max(peaks[rows], axis=1, keepdims=True)
                kept_peak[i, r, rows] = jnp.broadcast_to(peak, (BLK, BLK))
            kept_mix[i, r] = mix_tile(scores, kept_peak.at[i, r], weights, va_of(r))
            if r == 0:
                @pl.when(g == 1)
                def _():
                    send_far(2)
                    send_near(3)
                    send_own(3)

                @pl.when(g == 2)
                def _():
                    pass_out(0, 1)

                @pl.when(g == 3)
                def _():
                    pass_out(0, 2)
        return p

    def far_part(i, p):
        g = EARLY * p + i

        @pl.when(g == 2)
        def _():
            pass_out(1, 2)

        gathered(g)
        bring(g, far_slots, va_far)

        score(g, 0, far_slots, None)
        for r in range(2):
            if r == 0:
                score(g, 1, far_slots, None)
            scores, peaks, weights = sides[r]
            for t in range(0, TILE, BLK):
                rows = slice(t, t + BLK)
                peak = jnp.max(peaks[rows], axis=1, keepdims=True)
                peaks[rows] = jnp.maximum(kept_peak[i, r, rows], peak)
            far_mix[...] = mix_tile(scores, peaks, weights, va_far)
            for h in range(WIDTH):
                rows = slice(h * BLK, h * BLK + BLK)
                factor = jnp.exp2((kept_peak[i, r, rows] - peaks[rows]) * SCALE)
                mixed = far_mix[rows, :D] + kept_mix[i, r, rows, :D] * factor
                total = far_mix[rows, D:] + kept_mix[i, r, rows, D:] * factor
                done[g, r * BLK : r * BLK + BLK, h * D : h * D + D] = (mixed / total).astype(jnp.bfloat16)

            @pl.when(g < EARLY)
            def _():
                out_copy(g, r, at(after, z, y)).start()
                if r == 1:
                    long_out(g, 0).start()

            @pl.when(g >= EARLY)
            def _():
                out_copy(g, r, None).start()
        return p

    def pair(p, carry):
        lax.fori_loop(0, 2, near_part, p)
        lax.fori_loop(0, 2, far_part, p)
        return carry

    lax.fori_loop(0, 2, pair, 0)

    for g in early:
        early_kv(g).wait_send()
        early_q(g).wait_send()
        for r in range(2):
            out_copy(g, r, None).wait()
    for step in range(3):
        long_q(step).wait_send()
    for g in range(EARLY):
        for r in range(2):
            out_copy(g, r, at(after, z, y)).wait()
        for step in range(3):
            long_out(g, step).wait_send()
        long_out(g, 2).wait_recv()

    def finish(g, carry):
        for src, cond in z_pairs():
            @pl.when(cond)
            def _():
                to_z(g, src).wait_send()
        for src, dst, dy, cond in y_own() + y_near() + y_far():
            @pl.when(cond)
            def _():
                to_y(g, src, dst, dy).wait_send()
        each_pass(g, lambda copy: copy.wait_send())
        return carry

    lax.fori_loop(0, GROUPS, finish, 0)


def local(queries, key_heads, section_values, block_docs):
    bf16, f32 = jnp.bfloat16, jnp.float32
    anywhere = pl.BlockSpec(memory_space=pl.ANY)
    late = GROUPS - EARLY
    dma = pltpu.SemaphoreType.DMA
    out = pl.pallas_call(
        kernel,
        out_shape=jax.ShapeDtypeStruct((TOK, HEADS * D), bf16),
        in_specs=[pl.BlockSpec(memory_space=pltpu.SMEM), anywhere, anywhere, anywhere],
        out_specs=anywhere,
        scratch_shapes=[
            pltpu.VMEM((TOK * HEADS, D), bf16),
            pltpu.VMEM((TOK * GROUPS, D), bf16),
            pltpu.VMEM((TOK * GROUPS, D), bf16),
            pltpu.VMEM((TOK * HEADS, D), f32),
            pltpu.VMEM((HEADS + late * WIDTH, TOK, D), bf16),
            pltpu.VMEM((late, 2, TOK, D), bf16),
            pltpu.VMEM((GROUPS, 9, 2, TOK, D), bf16),
            pltpu.VMEM((NEAR + BLK, 2 * D), bf16),
            pltpu.VMEM((FAR, 2 * D), bf16),
            pltpu.VMEM((TILE, NEAR), f32),
            pltpu.VMEM((TILE, NEAR), f32),
            pltpu.VMEM((TILE, BLK), f32),
            pltpu.VMEM((TILE, BLK), f32),
            pltpu.VMEM((TILE, NEAR), bf16),
            pltpu.VMEM((TILE, NEAR), bf16),
            pltpu.VMEM((2, 2, TILE, 2 * D), f32),
            pltpu.VMEM((2, 2, TILE, D), f32),
            pltpu.VMEM((TILE, 2 * D), f32),
            pltpu.VMEM((GROUPS, TOK, WIDTH * D), bf16),
            pltpu.VMEM((2, LONG, TOK, D), bf16),
            pltpu.VMEM((EARLY, 2, TOK, LONG * D), bf16),
            dma((3,)),
            dma((GROUPS, 9)),
            dma((GROUPS, 9)),
            dma((GROUPS, 2, 2)),
            dma((GROUPS, 2, 2)),
            dma((late,)),
            dma((late,)),
            dma((late,)),
            dma((late,)),
            dma((3,)),
            dma((3,)),
            dma((EARLY, 3)),
            dma((EARLY, 3)),
            dma((EARLY, 2)),
            dma((EARLY, 2)),
            dma((GROUPS, 2)),
        ],
        compiler_params=pltpu.CompilerParams(
            collective_id=0, has_side_effects=True, vmem_limit_bytes=60 * MIB
        ),
    )(
        block_docs,
        queries.reshape(TOK * HEADS, D),
        key_heads.reshape(TOK * GROUPS, D),
        section_values.reshape(TOK * GROUPS, D),
    )
    return out[None]


def solution(mesh):
    specs = P("section", "ctx", "tp", None)
    return jax.shard_map(
        local,
        mesh=mesh,
        in_specs=(specs, specs, specs, P()),
        out_specs=P("section", "ctx", "tp"),
        check_vma=False,
    )
```

```python
import functools
import math

import jax
import jax.numpy as jnp
from jax import lax
from jax.experimental import pallas as pl
from jax.experimental.pallas import tpu as pltpu
from jax.sharding import PartitionSpec as P

MESH = pl.DeviceIdType.MESH
MIB = 1 << 20
BLK = 128
TOK = 256
D = 128
GROUPS = 4
WIDTH = 8
HEADS = GROUPS * WIDTH
NEAR = 11 * BLK
FAR = 4 * BLK
TILE = 1024
PER_TILE = TILE // BLK
CHUNK = 256
NY = 4
NZ = 8
NX = 4
EARLY = 2
LONG = 2
SHORT = WIDTH - LONG
LOW_SCORE = -1e30
SCALE = math.log2(math.e) / math.sqrt(D)


def score_tile(q, pieces, scores, peaks, causal):
    peak, c = None, 0
    for i, (keys, added) in enumerate(pieces):
        s = lax.dot_general(
            q, keys, (((1,), (1,)), ((), ())), preferred_element_type=jnp.float32
        )
        for b, bias in enumerate(added):
            part = s[:, b * BLK : b * BLK + BLK]
            if causal is not None and i + 1 == len(pieces) and b + 1 == len(added):
                part = jnp.where(causal, part, LOW_SCORE)
            else:
                part = part + bias
            scores[:, c : c + BLK] = part
            peak = part if peak is None else jnp.maximum(peak, part)
            c += BLK
    peaks[...] = peak


def mix_tile(scores, peaks, weights, va):
    keys = va.shape[0]
    for t in range(0, TILE, BLK):
        rows = slice(t, t + BLK)
        peak = peaks[rows]
        for c in range(0, keys, BLK):
            part = jnp.exp2((scores[rows, c : c + BLK] - peak) * SCALE)
            weights[rows, c : c + BLK] = part.astype(jnp.bfloat16)
    return jnp.dot(weights[:, :keys], va[...], preferred_element_type=jnp.float32)


def kernel(
    docs, q_hbm, k_hbm, v_hbm, out_hbm,
    q_in, k_in, v_in, wide, heads, first, kv, va_near, va_far,
    scores_a, scores_b, peaks_a, peaks_b, weights_a, weights_b, kept_mix, kept_peak, far_mix, done, hop_q, hop_o,
    in_sem, g_send, g_recv, f_recv, r_send, r_recv, k_send, k_recv, q_send, q_recv, hq_send, hq_recv,
    ho_send, ho_recv, x_send, x_recv, l_sem,
):
    sec, ctx, tp = lax.axis_index("section"), lax.axis_index("ctx"), lax.axis_index("tp")
    z, y = ctx // NY, ctx % NY
    after, before = (sec + 1) % NX, (sec + NX - 1) % NX

    def at(s, zz, yy):
        return (s, zz * NY + yy, tp)

    load_k = pltpu.make_async_copy(k_hbm, k_in, in_sem.at[0])
    load_v = pltpu.make_async_copy(v_hbm, v_in, in_sem.at[1])
    load_q = pltpu.make_async_copy(q_hbm, q_in, in_sem.at[2])
    load_k.start()
    load_v.start()
    load_q.start()

    barrier = pltpu.get_barrier_semaphore()
    peers = [at(after, z, y), at(before, z, y)]
    peers += [at(sec, z, (y + i) % NY) for i in (1, NY - 1)]
    peers += [at(sec, (z + i) % NZ, y) for i in (1, NZ - 1)]
    for peer in peers:
        pl.semaphore_signal(barrier, inc=1, device_id=peer, device_id_type=MESH)

    for i, (load, source) in enumerate(((load_k, k_in), (load_v, v_in))):
        load.wait()
        rows = TOK * GROUPS
        wide[:rows] = source[...].astype(jnp.float32)
        for g in range(GROUPS):
            part = wide[pl.ds(g, TOK, stride=GROUPS), :].astype(jnp.bfloat16)
            if g < EARLY:
                kv[g, 0, i] = part
            else:
                first[g - EARLY, i] = part

    pl.semaphore_wait(barrier, len(peers))

    def remote(src, dst, ssem, rsem, peer):
        return pltpu.make_async_remote_copy(
            src_ref=src, dst_ref=dst, send_sem=ssem, recv_sem=rsem,
            device_id=peer, device_id_type=MESH,
        )

    def block_copy(g, src_slot, dst_slot, send_slot, peer):
        return remote(
            kv.at[g, src_slot], kv.at[g, dst_slot], g_send.at[g, send_slot],
            g_recv.at[g, dst_slot], peer,
        )

    def to_z(g, src_slot):
        return block_copy(g, src_slot, src_slot + 4, src_slot // 4, at(sec, (z + 1) % NZ, y))

    def to_y(g, src_slot, dst_slot, dy):
        return block_copy(g, src_slot, dst_slot, dst_slot + (1 if dst_slot < 4 else 0), at(sec, z, (y + dy) % NY))

    def z_pairs():
        onward = jnp.logical_and(z >= 1, jnp.logical_and(z < NZ - 1, y > 0))
        return ((0, z < NZ - 1), (4, onward))

    def y_own():
        return [(0, dy, dy, y + dy < NY) for dy in (1, NY - 1)]

    def y_near():
        near = [(4, 4 + dy, dy, jnp.logical_and(z >= 1, y + dy < NY)) for dy in (1, NY - 1)]
        return near + [(4, dy, dy, jnp.logical_and(z >= 1, y + dy >= NY)) for dy in (1, NY - 1)]

    def y_far():
        return [(8, 4 + dy, dy, jnp.logical_and(z >= 2, y + dy >= NY)) for dy in (1, NY - 1)]

    def arrived(g, slot, cond):
        @pl.when(cond)
        def _():
            block_copy(g, slot, slot, 0, at(after, z, y)).wait_recv()

    def send_z(g, which):
        src, cond = z_pairs()[which]

        @pl.when(cond)
        def _():
            to_z(g, src).start()

    def send_y(g, which):
        for src, dst, dy, cond in which:
            @pl.when(cond)
            def _():
                to_y(g, src, dst, dy).start()

    def send_own(g):
        send_y(g, y_own())

    def send_near(g):
        arrived(g, 4, z >= 1)
        send_z(g, 1)
        send_y(g, y_near())

    def send_far(g):
        arrived(g, 8, jnp.logical_and(z >= 2, y > 0))
        send_y(g, y_far())

    passes = (
        (0, 0, 5, 6, 1, 2), (0, 0, 1, 2, 1, 1), (0, 0, 3, 6, -1, 1), (0, 1, 3, 6, -1, 1),
        (1, 0, 1, 2, 1, 0), (1, 0, 7, 6, -1, 2), (1, 1, 7, 6, -1, 2), (1, 0, 5, 6, 1, 1),
        (2, 0, 1, 2, 1, 0), (2, 1, 1, 2, 1, 0), (2, 1, 7, 6, -1, 2), (2, 1, 3, 2, -1, 1),
        (3, 1, 3, 2, -1, 0), (3, 1, 7, 6, -1, 1), (3, 0, 5, 2, 1, 1), (3, 1, 5, 2, 1, 1),
    )

    def pass_copy(g, part, here, there, dy):
        return remote(
            kv.at[g, here, part], kv.at[g, there, part], r_send.at[g, there // 4, part],
            r_recv.at[g, there // 4, part], at(sec, z, (y + NY + dy) % NY),
        )

    def each_pass(g, act):
        for i in range(4):
            for who, part, here, there, dy, least in passes[i::4]:
                @pl.when(jnp.logical_and(y == who, z >= least))
                def _():
                    act(pass_copy(g, part, here, there, dy))

    def relay_again(g):
        for slot in (1, 3, 5, 7):
            arrived(g, slot, ctx >= slot)
        each_pass(g, lambda copy: copy.start())

    def gathered(g):
        for slot in (2, 6):
            @pl.when(ctx >= slot)
            def _():
                for part in range(2):
                    pass_copy(g, part, slot, slot, 1).wait_recv()

    def early_kv(g):
        return remote(
            first.at[g - EARLY], kv.at[g, 0], k_send.at[g - EARLY], k_recv.at[g - EARLY],
            at(after, z, y),
        )

    moved = EARLY * WIDTH

    def early_q(g):
        count = WIDTH if g == EARLY else SHORT
        return remote(
            heads.at[pl.ds(g * WIDTH, count)], heads.at[pl.ds(g * WIDTH + moved, count)],
            q_send.at[g - EARLY], q_recv.at[g - EARLY], at(after, z, y),
        )

    def long_q(step):
        own = (GROUPS - 1) * WIDTH + SHORT
        src = heads.at[pl.ds(own, LONG)] if step == 0 else hop_q.at[step - 1]
        dst = heads.at[pl.ds(own + moved, LONG)] if step == 2 else hop_q.at[step]
        return remote(src, dst, hq_send.at[step], hq_recv.at[step], at(before, z, y))

    def long_out(g, step):
        cols = pl.ds(SHORT * D, LONG * D)
        far_cols = pl.ds(pl.multiple_of(g * WIDTH * D + SHORT * D, LONG * D), LONG * D)
        src = done.at[g, :, cols] if step == 0 else hop_o.at[g, step - 1]
        dst = out_hbm.at[:, far_cols] if step == 2 else hop_o.at[g, step]
        return remote(src, dst, ho_send.at[g, step], ho_recv.at[g, step], at(before, z, y))

    def pass_q(step):
        long_q(step - 1).wait_recv()
        long_q(step).start()

    def pass_out(g, step):
        long_out(g, step - 1).wait_recv()
        long_out(g, step).start()

    def part_copy(part, src_slot, dst_slot, send_slot, rsem, peer):
        return remote(kv.at[0, src_slot, part], kv.at[0, dst_slot, part], g_send.at[0, send_slot], rsem, peer)

    def first_z(part):
        return part_copy(part, 0, 4, 0, f_recv.at[part], at(sec, (z + 1) % NZ, y))

    def first_near(part):
        @pl.when(z >= 1)
        def _():
            first_z(part).wait_recv()

        @pl.when(z_pairs()[1][1])
        def _():
            part_copy(part, 4, 8, 1, g_recv.at[0, 8], at(sec, (z + 1) % NZ, y)).start()

        for src, dst, dy, cond in y_near():
            @pl.when(cond)
            def _():
                send_slot = dst + (1 if dst < 4 else 0)
                peer = at(sec, z, (y + dy) % NY)
                part_copy(part, src, dst, send_slot, g_recv.at[0, dst], peer).start()

    early = range(EARLY, GROUPS)

    @pl.when(z < NZ - 1)
    def _():
        for part in range(2):
            first_z(part).start()

    send_own(0)
    send_z(1, 0)
    for g in early:
        early_kv(g).start()
    load_q.wait()
    wide[...] = q_in[...].astype(jnp.float32)
    for h in range(moved, HEADS):
        heads[h] = wide[pl.ds(h, TOK, stride=HEADS), :].astype(jnp.bfloat16)
        if (h + 1) % WIDTH == 0:
            early_q(h // WIDTH).start()
        if h == HEADS - 1:
            long_q(0).start()
    for part in range(2):
        first_near(part)
    send_own(1)
    send_near(1)
    for h in range(moved):
        heads[h] = wide[pl.ds(h, TOK, stride=HEADS), :].astype(jnp.bfloat16)
    va_near[:, D:] = jnp.ones((NEAR + BLK, D), jnp.bfloat16)
    va_far[:, D:] = jnp.ones((FAR, D), jnp.bfloat16)
    for slot in range(1, 8):
        @pl.when(ctx < slot)
        def _():
            for g in range(GROUPS):
                kv[g, slot] = jnp.zeros((2, TOK, D), jnp.bfloat16)

    early_kv(2).wait_recv()
    send_z(2, 0)
    early_kv(3).wait_recv()
    send_z(3, 0)
    send_far(0)
    pass_q(1)
    send_far(1)

    row = lax.broadcasted_iota(jnp.int32, (BLK, BLK), 0)
    col = lax.broadcasted_iota(jnp.int32, (BLK, BLK), 1)
    causal = jnp.concatenate([row >= col] * PER_TILE, axis=0)

    def out_copy(g, r, peer):
        width = WIDTH * D if peer is None else SHORT * D
        src = done.at[g, pl.ds(r * BLK, BLK), pl.ds(0, width)]
        dst = out_hbm.at[pl.ds(r * BLK, BLK), pl.ds(pl.multiple_of(g * WIDTH * D, WIDTH * D), width)]
        if peer is None:
            return pltpu.make_async_copy(src, dst, l_sem.at[g, r])
        return remote(src, dst, x_send.at[g, r], x_recv.at[g, r], peer)

    near_slots, far_slots = (7, 1, 3, 4, 5, 0), (2, 6)

    def bring(g, slots, va):
        for i, slot in enumerate(slots):
            va[i * TOK : i * TOK + TOK, :D] = kv[g, slot, 1]

    def pieces_of(g, r, slots):
        mine = docs[2 * ctx + r]
        pieces = []
        for slot in slots:
            halves = (0,) if (slot, r) == (0, 0) else (1,) if (slot, r) == (7, 1) else (0, 1)
            keys = kv[g, slot, 0, halves[0] * BLK : halves[-1] * BLK + BLK]
            added = []
            for half in halves:
                block = 2 * (ctx - slot) + half
                ok = jnp.logical_and(block >= 0, docs[jnp.maximum(block, 0)] == mine)
                added.append(jnp.where(ok, 0.0, LOW_SCORE).astype(jnp.float32))
            pieces.append((keys, added))
        return pieces

    def va_of(r):
        return va_near.at[r * BLK : r * BLK + NEAR]

    sides = ((scores_a, peaks_a, weights_a), (scores_b, peaks_b, weights_b))

    def score(g, r, slots, mask):
        base = g * WIDTH + (g // EARLY) * moved
        q = heads[pl.ds(base, WIDTH), r * BLK : r * BLK + BLK].reshape(TILE, D)
        scores, peaks, _ = sides[r]
        score_tile(q, pieces_of(g, r, slots), scores, peaks, mask)

    def near_part(i, p):
        g = EARLY * p + i

        @pl.when(g == 2)
        def _():
            send_far(3)

        for slot in (1, 3, 5, 7):
            arrived(g, slot, ctx >= slot)
        each_pass(g, lambda copy: copy.start())

        @pl.when(g == 0)
        def _():
            send_near(2)
            send_own(2)
            pass_q(2)

        @pl.when(g == 1)
        def _():
            send_near(3)
            send_own(3)

        @pl.when(g == 2)
        def _():
            early_q(2).wait_recv()

        @pl.when(g == 3)
        def _():
            pass_out(1, 1)
            early_q(3).wait_recv()
            long_q(2).wait_recv()

        bring(g, near_slots, va_near)

        score(g, 0, near_slots, causal)
        for r in range(2):
            if r == 0:
                score(g, 1, near_slots, causal)
            scores, peaks, weights = sides[r]
            for t in range(0, TILE, BLK):
                rows = slice(t, t + BLK)
                peak = jnp.max(peaks[rows], axis=1, keepdims=True)
                kept_peak[i, r, rows] = jnp.broadcast_to(peak, (BLK, BLK))
            kept_mix[i, r] = mix_tile(scores, kept_peak.at[i, r], weights, va_of(r))
            if r == 0:
                @pl.when(g == 1)
                def _():
                    send_far(2)

                @pl.when(g == 2)
                def _():
                    pass_out(0, 1)

                @pl.when(g == 3)
                def _():
                    pass_out(0, 2)
        return p

    def far_part(i, p):
        g = EARLY * p + i

        @pl.when(g == 2)
        def _():
            pass_out(1, 2)

        gathered(g)
        bring(g, far_slots, va_far)

        score(g, 0, far_slots, None)
        for r in range(2):
            if r == 0:
                score(g, 1, far_slots, None)
            scores, peaks, weights = sides[r]
            for t in range(0, TILE, BLK):
                rows = slice(t, t + BLK)
                peak = jnp.max(peaks[rows], axis=1, keepdims=True)
                peaks[rows] = jnp.maximum(kept_peak[i, r, rows], peak)
            far_mix[...] = mix_tile(scores, peaks, weights, va_far)
            for h in range(WIDTH):
                rows = slice(h * BLK, h * BLK + BLK)
                factor = jnp.exp2((kept_peak[i, r, rows] - peaks[rows]) * SCALE)
                mixed = far_mix[rows, :D] + kept_mix[i, r, rows, :D] * factor
                total = far_mix[rows, D:] + kept_mix[i, r, rows, D:] * factor
                done[g, r * BLK : r * BLK + BLK, h * D : h * D + D] = (mixed / total).astype(jnp.bfloat16)

            @pl.when(g < EARLY)
            def _():
                out_copy(g, r, at(after, z, y)).start()
                if r == 1:
                    long_out(g, 0).start()

            @pl.when(g >= EARLY)
            def _():
                out_copy(g, r, None).start()
        return p

    def pair(p, carry):
        lax.fori_loop(0, 2, near_part, p)
        lax.fori_loop(0, 2, far_part, p)
        return carry

    lax.fori_loop(0, 2, pair, 0)

    for g in early:
        early_kv(g).wait_send()
        early_q(g).wait_send()
        for r in range(2):
            out_copy(g, r, None).wait()
    for step in range(3):
        long_q(step).wait_send()
    for g in range(EARLY):
        for r in range(2):
            out_copy(g, r, at(after, z, y)).wait()
        for step in range(3):
            long_out(g, step).wait_send()
        long_out(g, 2).wait_recv()

    def finish(g, carry):
        for src, cond in z_pairs():
            @pl.when(cond)
            def _():
                to_z(g, src).wait_send()
        for src, dst, dy, cond in y_own() + y_near() + y_far():
            @pl.when(cond)
            def _():
                to_y(g, src, dst, dy).wait_send()
        each_pass(g, lambda copy: copy.wait_send())
        return carry

    lax.fori_loop(0, GROUPS, finish, 0)


def local(queries, key_heads, section_values, block_docs):
    bf16, f32 = jnp.bfloat16, jnp.float32
    anywhere = pl.BlockSpec(memory_space=pl.ANY)
    late = GROUPS - EARLY
    dma = pltpu.SemaphoreType.DMA
    out = pl.pallas_call(
        kernel,
        out_shape=jax.ShapeDtypeStruct((TOK, HEADS * D), bf16),
        in_specs=[pl.BlockSpec(memory_space=pltpu.SMEM), anywhere, anywhere, anywhere],
        out_specs=anywhere,
        scratch_shapes=[
            pltpu.VMEM((TOK * HEADS, D), bf16),
            pltpu.VMEM((TOK * GROUPS, D), bf16),
            pltpu.VMEM((TOK * GROUPS, D), bf16),
            pltpu.VMEM((TOK * HEADS, D), f32),
            pltpu.VMEM((HEADS + late * WIDTH, TOK, D), bf16),
            pltpu.VMEM((late, 2, TOK, D), bf16),
            pltpu.VMEM((GROUPS, 9, 2, TOK, D), bf16),
            pltpu.VMEM((NEAR + BLK, 2 * D), bf16),
            pltpu.VMEM((FAR, 2 * D), bf16),
            pltpu.VMEM((TILE, NEAR), f32),
            pltpu.VMEM((TILE, NEAR), f32),
            pltpu.VMEM((TILE, BLK), f32),
            pltpu.VMEM((TILE, BLK), f32),
            pltpu.VMEM((TILE, NEAR), bf16),
            pltpu.VMEM((TILE, NEAR), bf16),
            pltpu.VMEM((2, 2, TILE, 2 * D), f32),
            pltpu.VMEM((2, 2, TILE, D), f32),
            pltpu.VMEM((TILE, 2 * D), f32),
            pltpu.VMEM((GROUPS, TOK, WIDTH * D), bf16),
            pltpu.VMEM((2, LONG, TOK, D), bf16),
            pltpu.VMEM((EARLY, 2, TOK, LONG * D), bf16),
            dma((3,)),
            dma((GROUPS, 9)),
            dma((GROUPS, 9)),
            dma((2,)),
            dma((GROUPS, 2, 2)),
            dma((GROUPS, 2, 2)),
            dma((late,)),
            dma((late,)),
            dma((late,)),
            dma((late,)),
            dma((3,)),
            dma((3,)),
            dma((EARLY, 3)),
            dma((EARLY, 3)),
            dma((EARLY, 2)),
            dma((EARLY, 2)),
            dma((GROUPS, 2)),
        ],
        compiler_params=pltpu.CompilerParams(
            collective_id=0, has_side_effects=True, vmem_limit_bytes=60 * MIB
        ),
    )(
        block_docs,
        queries.reshape(TOK * HEADS, D),
        key_heads.reshape(TOK * GROUPS, D),
        section_values.reshape(TOK * GROUPS, D),
    )
    return out[None]


def solution(mesh):
    specs = P("section", "ctx", "tp", None)
    return jax.shard_map(
        local,
        mesh=mesh,
        in_specs=(specs, specs, specs, P()),
        out_specs=P("section", "ctx", "tp"),
        check_vma=False,
    )
```
